32 devices in a mesh: dp: 8 (over z, x), tensor: 4 (over y, core).
Axes of the slice: x: 2, y: 2, z: 4, core: 2. Of those that a mesh axis runs over, the one named last changes fastest.
Arguments:
- states: bfloat16 [8, 1024, 768], P('dp', 'tensor'), may hold values from -6 to 6
- encoder: bfloat16 [8, 512, 768], P('dp', 'tensor'), may hold values from -6 to 6
- upstream: bfloat16 [8, 1024, 768], P('dp', 'tensor'), may hold values from -6 to 6
- decoder_docs: int32 [8, 1024], P('dp'), may hold values from 0 to 3, as said below
- encoder_docs: int32 [8, 512], P('dp'), may hold values from 0 to 3, as said below
- norm_self: float32 [768], replicated, may hold values from 0.25 to 1.75
- norm_cross: float32 [768], replicated, may hold values from 0.25 to 1.75
- norm_feed: float32 [768], replicated, may hold values from 0.25 to 1.75
- position_table: float32 [32, 12], replicated, may hold values from -4 to 4
- self_query: bfloat16 [768, 768], P('dp', 'tensor'), may hold values from -0.0546875 to 0.0546875
- self_key: bfloat16 [768, 768], P('dp', 'tensor'), may hold values from -0.21875 to 0.21875
- self_value: bfloat16 [768, 768], P('dp', 'tensor'), may hold values from -0.21875 to 0.21875
- self_output: bfloat16 [768, 768], P('tensor', 'dp'), may hold values from -0.625 to 0.625
- cross_query: bfloat16 [768, 768], P('dp', 'tensor'), may hold values from -0.0546875 to 0.0546875
- cross_key: bfloat16 [768, 768], P('dp', 'tensor'), may hold values from -0.21875 to 0.21875
- cross_value: bfloat16 [768, 768], P('dp', 'tensor'), may hold values from -0.21875 to 0.21875
- cross_output: bfloat16 [768, 768], P('tensor', 'dp'), may hold values from -0.625 to 0.625
- feed_gate: bfloat16 [768, 2048], P('dp', 'tensor'), may hold values from -0.21875 to 0.21875
- feed_up: bfloat16 [768, 2048], P('dp', 'tensor'), may hold values from -0.21875 to 0.21875
- feed_down: bfloat16 [2048, 768], P('tensor', 'dp'), may hold values from -0.125 to 0.125
Outputs:
- layer_output: bfloat16 [8, 1024, 768], P('dp', 'tensor')
- states_gradient: float32 [8, 1024, 768], P('dp', 'tensor')
- encoder_gradient: float32 [8, 512, 768], P('dp', 'tensor')
- norm_self_gradient: float32 [768], replicated
- norm_cross_gradient: float32 [768], replicated
- norm_feed_gradient: float32 [768], replicated
- table_gradient: float32 [32, 12], replicated
- self_query_gradient: float32 [768, 768], P('dp', 'tensor')
- self_key_gradient: float32 [768, 768], P('dp', 'tensor')
- self_value_gradient: float32 [768, 768], P('dp', 'tensor')
- self_output_gradient: float32 [768, 768], P('tensor', 'dp')
- cross_query_gradient: float32 [768, 768], P('dp', 'tensor')
- cross_key_gradient: float32 [768, 768], P('dp', 'tensor')
- cross_value_gradient: float32 [768, 768], P('dp', 'tensor')
- cross_output_gradient: float32 [768, 768], P('tensor', 'dp')
- feed_gate_gradient: float32 [768, 2048], P('dp', 'tensor')
- feed_up_gradient: float32 [768, 2048], P('dp', 'tensor')
- feed_down_gradient: float32 [2048, 768], P('tensor', 'dp')
The draws below stay inside these ranges and needn't reach their ends.
Inputs may be any that keep to these rules, and one draw needn't show every extreme that they name: `decoder_docs`: along each sequence the ids never fall; every sequence holds each of the ids 0, 1, 2, 3, each over 64 tokens or more. Decoder document d of a sequence reads encoder document d of the same sequence. `encoder_docs`: along each sequence the ids never fall; every sequence holds each of the ids 0, 1, 2, 3, each over 32 states or more.
All inputs are finite; a program needn't handle non-finite values.
Results may differ from the reference program's by a relative error of at most 0.023.
The reference program's roundings to bfloat16 on the way count: a program that leaves them out, or rounds other values in their place, can miss the bound.
Values may be sent and summed in bfloat16 or wider, within the bound.
A program may use at most 128 MiB of HBM per device.

```python
import math
import jax
import jax.numpy as jnp
from jax import lax

D = 768
HEADS = 12
HEAD_DIM = 64
FF = 2048
BUCKETS = 32
LEN = 1024
ENC_LEN = 512
SEQS = 8
SPLIT_ROWS = 256
ENC_ROWS = 128


def document_ids(key, length, quarter):
    shortest = max(length // 16, 1)
    parts = jax.random.split(key, 3)
    first = jax.random.randint(parts[0], (), shortest, quarter)
    second = jax.random.randint(parts[1], (), length - quarter + 1, length - 2 * shortest + 1)
    third = jax.random.randint(parts[2], (), second + shortest, length - shortest + 1)
    places = jnp.arange(length, dtype=jnp.int32)
    return (places >= first).astype(jnp.int32) + (places >= second).astype(jnp.int32) + (places >= third).astype(jnp.int32)


def draw_decoder_docs(key, part):
    key = jax.random.fold_in(key, 5)
    return jax.vmap(lambda single: document_ids(single, LEN, SPLIT_ROWS))(jax.random.split(key, SEQS))


def draw_encoder_docs(key, part):
    key = jax.random.fold_in(key, 9)
    return jax.vmap(lambda single: document_ids(single, ENC_LEN, ENC_ROWS))(jax.random.split(key, SEQS))


def level_of(own_key, dims, shards, smallest, high):
    def one(axis_at, blocks):
        steps = jax.random.uniform(jax.random.fold_in(jax.random.fold_in(own_key, 6), axis_at), (blocks,), jnp.float32, smallest / len(shards), high / len(shards))
        return jnp.repeat(jnp.exp(steps), dims[axis_at] // blocks).reshape((-1,) + (1,) * (len(dims) - axis_at - 1))

    factor_of = one(*shards[0])
    for cut in shards[1:]:
        factor_of = factor_of * one(*cut)
    return factor_of


def gaussian(own_key, dims, deviation, bound, shards=(), held_as=jnp.bfloat16):
    array = deviation * jax.random.normal(own_key, dims, jnp.float32)
    if shards:
        array = array * level_of(own_key, dims, shards, -0.22, 0.18)
    return jnp.clip(array, -bound, bound).astype(held_as)


def setup_inputs(seed: int = 0) -> dict:
    key_list = jax.random.split(jax.random.key(seed), 21)
    states = gaussian(key_list[0], (SEQS, LEN, D), 1.0, 6.0, ((0, 8), (1, 4)))
    encoder = gaussian(key_list[1], (SEQS, ENC_LEN, D), 1.0, 6.0, ((0, 8), (1, 4)))
    upstream = gaussian(key_list[2], (SEQS, LEN, D), 1.0, 6.0, ((0, 8), (1, 4)))
    decoder_docs = draw_decoder_docs(jax.random.fold_in(key_list[20], 71), 0)
    encoder_docs = draw_encoder_docs(jax.random.fold_in(key_list[20], 71), 0)
    norm_self = jnp.clip(1.0 + 0.15 * jax.random.normal(key_list[5], (D,), jnp.float32), 0.25, 1.75)
    norm_cross = jnp.clip(1.0 + 0.15 * jax.random.normal(key_list[6], (D,), jnp.float32), 0.25, 1.75)
    norm_feed = jnp.clip(1.0 + 0.15 * jax.random.normal(key_list[7], (D,), jnp.float32), 0.25, 1.75)
    position_table = gaussian(key_list[8], (BUCKETS, HEADS), 1.0, 4.0, (), jnp.float32)
    self_query = gaussian(key_list[9], (D, D), (D * HEAD_DIM // 4) ** -0.5, 0.0546875, ((0, 8), (1, 4)))
    self_key = gaussian(key_list[10], (D, D), D ** -0.5, 0.21875, ((0, 8), (1, 4)))
    self_value = gaussian(key_list[11], (D, D), D ** -0.5, 0.21875, ((0, 8), (1, 4)))
    self_output = gaussian(key_list[12], (D, D), (D // 8) ** -0.5, 0.625, ((0, 4), (1, 8)))
    cross_query = gaussian(key_list[13], (D, D), (D * HEAD_DIM // 4) ** -0.5, 0.0546875, ((0, 8), (1, 4)))
    cross_key = gaussian(key_list[14], (D, D), D ** -0.5, 0.21875, ((0, 8), (1, 4)))
    cross_value = gaussian(key_list[15], (D, D), D ** -0.5, 0.21875, ((0, 8), (1, 4)))
    cross_output = gaussian(key_list[16], (D, D), (D // 8) ** -0.5, 0.625, ((0, 4), (1, 8)))
    feed_gate = gaussian(key_list[17], (D, FF), D ** -0.5, 0.21875, ((0, 8), (1, 4)))
    feed_up = gaussian(key_list[18], (D, FF), D ** -0.5, 0.21875, ((0, 8), (1, 4)))
    feed_down = gaussian(key_list[19], (FF, D), FF ** -0.5, 0.125, ((0, 4), (1, 8)))
    return {"states": states, "encoder": encoder, "upstream": upstream, "decoder_docs": decoder_docs, "encoder_docs": encoder_docs, "norm_self": norm_self, "norm_cross": norm_cross, "norm_feed": norm_feed, "position_table": position_table, "self_query": self_query, "self_key": self_key, "self_value": self_value, "self_output": self_output, "cross_query": cross_query, "cross_key": cross_key, "cross_value": cross_value, "cross_output": cross_output, "feed_gate": feed_gate, "feed_up": feed_up, "feed_down": feed_down}


@jax.custom_vjp
def low(v):
    return lax.optimization_barrier(v.astype(jnp.bfloat16)).astype(jnp.float32)

@jax.custom_vjp
def low_back(v):
    return v

def low_keep(v):
    return (low(v), None)

def low_pass(kept, grad):
    return (grad,)

def back_keep(v):
    return (v, None)

def back_low(kept, grad):
    return (low(grad),)
low.defvjp(low_keep, low_pass)
low_back.defvjp(back_keep, back_low)
EPS = 1e-06
NEG = -1e+30
far_distance = 128

def bucket_edges():
    half = BUCKETS // 2
    upper = [int(math.ceil(half * (far_distance / half) ** (step / half))) for step in range(1, BUCKETS - half)]
    return list(range(1, half + 1)) + upper

def norm_rows(token_rows, gain):
    return token_rows * lax.rsqrt(lax.optimization_barrier(jnp.mean(token_rows * token_rows, -1, keepdims=True)) + EPS) * gain

def product(left, right):
    return jnp.matmul(left, right, precision=lax.Precision.HIGHEST)

def attention(query, keys, values, allowed, bias):
    length = query.shape[0]
    query = query.reshape(length, -1, HEAD_DIM)
    keys = keys.reshape(keys.shape[0], -1, HEAD_DIM)
    values = values.reshape(values.shape[0], -1, HEAD_DIM)
    scores = low_back(jnp.einsum('qhd,khd->hqk', query, keys, precision=lax.Precision.HIGHEST)) + bias
    shares = jax.nn.softmax(jnp.where(allowed[None], scores, NEG), axis=-1)
    mixed = jnp.einsum('hqk,khd->qhd', low(shares), values, precision=lax.Precision.HIGHEST)
    return low_back(low(mixed.reshape(length, -1)))

def layer(params, states, encoder, decoder_docs, encoder_docs):
    norm_self, norm_cross, norm_feed, table, self_query, self_key, self_value, self_output, cross_query, cross_key, cross_value, cross_output, feed_gate, feed_up, feed_down = params
    places = jnp.arange(LEN, dtype=jnp.int32)
    distance = jnp.maximum(places[:, None] - places[None, :], 0)
    buckets = jnp.zeros((LEN, LEN), jnp.int32)
    for edge in bucket_edges():
        buckets = buckets + (distance >= edge).astype(jnp.int32)
    bias = jnp.transpose(table[buckets], (2, 0, 1))
    causal = (decoder_docs[:, None] == decoder_docs[None, :]) & (places[:, None] >= places[None, :])
    matched = decoder_docs[:, None] == encoder_docs[None, :]
    normed = low(norm_rows(states, norm_self))
    query = low_back(low(product(normed, self_query)))
    keys = low_back(low(product(normed, self_key)))
    values = low_back(low(product(normed, self_value)))
    first = states + low_back(product(attention(query, keys, values, causal, bias), self_output))
    normed = low(norm_rows(first, norm_cross))
    query = low_back(low(product(normed, cross_query)))
    keys = low_back(low(product(encoder, cross_key)))
    values = low_back(low(product(encoder, cross_value)))
    second = first + low_back(product(attention(query, keys, values, matched, 0.0), cross_output))
    normed = low(norm_rows(second, norm_feed))
    gate_activation = low_back(product(normed, feed_gate))
    up_projection_output = low_back(product(normed, feed_up))
    hidden_state = low(jax.nn.gelu(gate_activation, approximate=True) * up_projection_output)
    return second + low_back(product(hidden_state, feed_down))

def reference(states, encoder, upstream, decoder_docs, encoder_docs, norm_self, norm_cross, norm_feed, position_table, self_query, self_key, self_value, self_output, cross_query, cross_key, cross_value, cross_output, feed_gate, feed_up, feed_down):
    params = tuple((value.astype(jnp.float32) for value in (norm_self, norm_cross, norm_feed, position_table, self_query, self_key, self_value, self_output, cross_query, cross_key, cross_value, cross_output, feed_gate, feed_up, feed_down)))

    def forward(decoder_rows, encoder_rows, weights):

        def one_sequence(items):
            return layer(weights, items[0], items[1], items[2], items[3])
        return lax.map(jax.checkpoint(one_sequence), (decoder_rows, encoder_rows, decoder_docs, encoder_docs))
    result, pullback = jax.vjp(forward, states.astype(jnp.float32), encoder.astype(jnp.float32), params)
    states_grad, encoder_grad, gradient_bundle = pullback(upstream.astype(jnp.float32))
    return (result.astype(jnp.bfloat16), states_grad, encoder_grad, gradient_bundle[0], gradient_bundle[1], gradient_bundle[2], gradient_bundle[3], gradient_bundle[4], gradient_bundle[5], gradient_bundle[6], gradient_bundle[7], gradient_bundle[8], gradient_bundle[9], gradient_bundle[10], gradient_bundle[11], gradient_bundle[12], gradient_bundle[13], gradient_bundle[14])
```

```python
import functools
import math

import jax
import jax.numpy as jnp
from jax import lax
from jax.experimental import pallas as pl
from jax.experimental.pallas import tpu as pltpu
from jax.sharding import PartitionSpec as P

HEADS = 12
HEAD_DIM = 64
BUCKETS = 32

EPS = 1e-06
NEG = -1e30
far_distance = 128


def bucket_edges():
    half = BUCKETS // 2
    upper = [
        int(math.ceil(half * (far_distance / half) ** (step / half)))
        for step in range(1, BUCKETS - half)
    ]
    return list(range(1, half + 1)) + upper


def distance_buckets(distance):
    count = jnp.zeros(distance.shape, jnp.int32)
    for edge in bucket_edges():
        count = count + (distance >= edge).astype(jnp.int32)
    return count


def dot(left, right, left_dim, right_dim):
    return lax.dot_general(
        left, right, (((left_dim,), (right_dim,)), ((), ())), preferred_element_type=jnp.float32
    )


def window_distance(shape, window, block):
    place = lax.broadcasted_iota(jnp.int32, shape, len(shape) - 1)
    return jnp.where(place > block, block + window - place, block - place)


def bias_window(table_ref, head, block):
    window = 2 * block
    distance = window_distance((8, window), window, block)
    count = distance_buckets(distance)
    line = jnp.zeros((8, window), jnp.float32)
    for bucket in range(BUCKETS):
        line = jnp.where(count == bucket, table_ref[head, bucket], line)
    row = lax.broadcasted_iota(jnp.int32, (8, window), 0)
    for step in (1, 2, 4):
        line = jnp.where((row & step) != 0, pltpu.roll(line, step, 1), line)
    step = 8
    while step < block:
        line = jnp.concatenate([line, pltpu.roll(line, step, 1)], 0)
        step = 2 * step
    return line


def diagonal_sums(tile, block):
    window = 2 * block
    step = block // 2
    while step >= 8:
        tile = tile[:step] + pltpu.roll(tile[step:], window - step, 1)
        step = step // 2
    row = lax.broadcasted_iota(jnp.int32, (8, window), 0)
    for step in (1, 2, 4):
        tile = jnp.where((row & step) != 0, pltpu.roll(tile, window - step, 1), tile)
    return jnp.sum(tile, 0, keepdims=True)


def self_scores(query, keys, docs_column, docs_row, index, block, table_ref, head, wide):
    size = (index + 1) * block
    raw = dot(query, keys[:size], 1, 1)
    parts = []
    for other in range(index + 1):
        piece = raw[:, other * block : (other + 1) * block]
        if other == index:
            piece = piece + wide[:, block:]
        elif other == index - 1:
            piece = piece + wide[:, :block]
        else:
            piece = piece + table_ref[head, BUCKETS - 1]
        same = docs_column == docs_row[:, other * block : (other + 1) * block]
        if other == index:
            place = lax.broadcasted_iota(jnp.int32, (block, block), 0)
            same = same & (place >= lax.broadcasted_iota(jnp.int32, (block, block), 1))
        parts.append(jnp.where(same, piece, NEG))
    return jnp.concatenate(parts, 1) if len(parts) > 1 else parts[0]


def softmax_mix(scores, values):
    top = jnp.max(scores, -1, keepdims=True)
    lifted = jnp.exp(scores - top)
    total = jnp.sum(lifted, -1, keepdims=True)
    shares = (lifted * (1.0 / total)).astype(jnp.bfloat16)
    return dot(shares, values, 1, 0).astype(jnp.bfloat16), top + jnp.log(total)


def head_slice(head):
    return slice(head * HEAD_DIM, (head + 1) * HEAD_DIM)


def self_forward_kernel(heads, block, table_ref, column_ref, row_ref, qkv_ref, mixed_ref, log_ref):
    width = heads * HEAD_DIM
    length = qkv_ref.shape[1]
    qkv = qkv_ref[0]
    docs_row = row_ref[0]
    mixed_heads, log_heads = [], []
    for head in range(heads):
        wide = bias_window(table_ref, head, block)
        cut = head_slice(head)
        query, keys, values = (
            qkv[:, part * width + cut.start : part * width + cut.stop] for part in range(3)
        )
        mixed_blocks, log_blocks = [], []
        for index in range(length // block):
            rows = slice(index * block, (index + 1) * block)
            scores = self_scores(
                query[rows], keys, column_ref[0, rows], docs_row, index, block, table_ref, head, wide
            )
            mixed, log_total = softmax_mix(scores, values[: rows.stop])
            mixed_blocks.append(mixed)
            log_blocks.append(log_total)
        mixed_heads.append(jnp.concatenate(mixed_blocks, 0))
        log_heads.append(jnp.concatenate(log_blocks, 0))
    mixed_ref[0] = jnp.concatenate(mixed_heads, 1)
    log_ref[0] = jnp.concatenate(log_heads, 1)


def self_backward_kernel(
    heads, block, table_ref, column_ref, row_ref, qkv_ref, log_ref, grad_ref, out_ref, diagonal_ref
):
    width = heads * HEAD_DIM
    length = qkv_ref.shape[1]
    window = 2 * block
    qkv = qkv_ref[0]
    grads = grad_ref[0]
    docs_row = row_ref[0]
    query_heads, key_heads, value_heads = [], [], []
    for head in range(heads):
        wide = bias_window(table_ref, head, block)
        cut = head_slice(head)
        query, keys, values = (
            qkv[:, part * width + cut.start : part * width + cut.stop] for part in range(3)
        )
        grad = grads[:, cut]
        blocks = length // block
        key_sums = [None] * blocks
        value_sums = [None] * blocks
        query_blocks = []
        near = jnp.zeros((block, block), jnp.float32)
        before = jnp.zeros((block, block), jnp.float32)
        far = jnp.zeros((1, block), jnp.float32)
        for index in range(blocks):
            rows = slice(index * block, (index + 1) * block)
            scores = self_scores(
                query[rows], keys, column_ref[0, rows], docs_row, index, block, table_ref, head, wide
            )
            shares = jnp.exp(scores - log_ref[0, rows, head : head + 1])
            share_grad = dot(grad[rows], values[: rows.stop], 1, 1)
            inner = jnp.sum(shares * share_grad, -1, keepdims=True)
            score_grad = shares * (share_grad - inner)
            low = score_grad.astype(jnp.bfloat16)
            query_blocks.append(dot(low, keys[: rows.stop], 1, 0).astype(jnp.bfloat16))
            key_part = dot(low, query[rows], 0, 0)
            value_part = dot(shares.astype(jnp.bfloat16), grad[rows], 0, 0)
            for other in range(index + 1):
                cols = slice(other * block, (other + 1) * block)
                key_sums[other] = (
                    key_part[cols] if key_sums[other] is None else key_sums[other] + key_part[cols]
                )
                value_sums[other] = (
                    value_part[cols]
                    if value_sums[other] is None
                    else value_sums[other] + value_part[cols]
                )
                if other == index:
                    near = near + score_grad[:, cols]
                elif other == index - 1:
                    before = before + score_grad[:, cols]
                else:
                    far = far + jnp.sum(score_grad[:, cols], 0, keepdims=True)
        line = diagonal_sums(jnp.concatenate([before, near], 1), block)
        place = lax.broadcasted_iota(jnp.int32, (1, window), 1)
        line = jnp.where(place == block + 1, line + jnp.sum(far), line)
        diagonal_ref[0, head : head + 1] = line
        query_heads.append(jnp.concatenate(query_blocks, 0))
        key_heads.append(jnp.concatenate(key_sums, 0).astype(jnp.bfloat16))
        value_heads.append(jnp.concatenate(value_sums, 0).astype(jnp.bfloat16))
    out_ref[0] = jnp.concatenate(query_heads + key_heads + value_heads, 1)


def cross_scores(query, keys, docs_column, docs_row):
    return jnp.where(docs_column == docs_row, dot(query, keys, 1, 1), NEG)


def cross_forward_kernel(heads, block, column_ref, row_ref, query_ref, both_ref, mixed_ref, log_ref):
    width = heads * HEAD_DIM
    both = both_ref[0]
    for index in range(query_ref.shape[1] // block):
        rows = slice(index * block, (index + 1) * block)
        mixed_heads, log_heads = [], []
        for head in range(heads):
            cut = head_slice(head)
            scores = cross_scores(
                query_ref[0, rows, cut], both[:, cut], column_ref[0, rows], row_ref[0]
            )
            mixed, log_total = softmax_mix(scores, both[:, width + cut.start : width + cut.stop])
            mixed_heads.append(mixed)
            log_heads.append(log_total)
        mixed_ref[0, rows] = jnp.concatenate(mixed_heads, 1)
        log_ref[0, rows] = jnp.concatenate(log_heads, 1)


def cross_backward_kernel(
    heads, block, column_ref, row_ref, query_ref, both_ref, log_ref, grad_ref, out_ref, both_out_ref
):
    width = heads * HEAD_DIM
    both = both_ref[0]
    query_heads, key_heads, value_heads = [], [], []
    for head in range(heads):
        cut = head_slice(head)
        keys = both[:, cut]
        values = both[:, width + cut.start : width + cut.stop]
        key_sum = value_sum = None
        query_blocks = []
        for index in range(query_ref.shape[1] // block):
            rows = slice(index * block, (index + 1) * block)
            query = query_ref[0, rows, cut]
            grad = grad_ref[0, rows, cut]
            scores = cross_scores(query, keys, column_ref[0, rows], row_ref[0])
            shares = jnp.exp(scores - log_ref[0, rows, head : head + 1])
            share_grad = dot(grad, values, 1, 1)
            inner = jnp.sum(shares * share_grad, -1, keepdims=True)
            low = (shares * (share_grad - inner)).astype(jnp.bfloat16)
            query_blocks.append(dot(low, keys, 1, 0).astype(jnp.bfloat16))
            key_part = dot(low, query, 0, 0)
            value_part = dot(shares.astype(jnp.bfloat16), grad, 0, 0)
            key_sum = key_part if key_sum is None else key_sum + key_part
            value_sum = value_part if value_sum is None else value_sum + value_part
        query_heads.append(jnp.concatenate(query_blocks, 0))
        key_heads.append(key_sum.astype(jnp.bfloat16))
        value_heads.append(value_sum.astype(jnp.bfloat16))
    out_ref[0] = jnp.concatenate(query_heads, 1)
    both_out_ref[0] = jnp.concatenate(key_heads + value_heads, 1)


def whole_block(value):
    shape = (1,) + value.shape[1:]
    return pl.BlockSpec(shape, lambda part: (part,) + (0,) * (len(shape) - 1))


def per_sequence(kernel, table, arrays, outs):
    ins = [whole_block(value) for value in arrays]
    operands = list(arrays)
    if table is not None:
        ins.insert(0, pl.BlockSpec(memory_space=pltpu.SMEM))
        operands.insert(0, table)
    return pl.pallas_call(
        kernel,
        grid=(arrays[0].shape[0],),
        in_specs=ins,
        out_specs=[whole_block(value) for value in outs],
        out_shape=outs,
        compiler_params=pltpu.CompilerParams(vmem_limit_bytes=56 * 1024 * 1024),
    )(*operands)


def norm_forward(rows, gain):
    scale = lax.rsqrt(jnp.mean(rows * rows, -1, keepdims=True) + EPS)
    return (rows * scale * gain).astype(jnp.bfloat16), scale


def norm_backward(rows, scale, gain, normed_grad):
    unit = rows * scale
    inward = normed_grad * gain
    rows_grad = scale * (inward - unit * jnp.mean(inward * unit, -1, keepdims=True))
    return rows_grad, jnp.sum(normed_grad * unit, (0, 1))


def gelu_parts(value):
    inner = math.sqrt(2 / math.pi) * (value + 0.044715 * value * value * value)
    curve = jnp.tanh(inner)
    activated = 0.5 * value * (1 + curve)
    slope = 0.5 * (1 + curve) + 0.5 * value * (1 - curve * curve) * math.sqrt(2 / math.pi) * (
        1 + 3 * 0.044715 * value * value
    )
    return activated, slope


def gather_rows(value):
    return lax.all_gather(value, "tensor", axis=1, tiled=True)


def scatter_rows(value):
    low = value.astype(jnp.bfloat16)
    return lax.psum_scatter(low, "tensor", scatter_dimension=1, tiled=True).astype(jnp.float32)


def gather_weight(pieces):
    return lax.all_gather(jnp.concatenate(pieces, 1), "dp", axis=0, tiled=True)


def scatter_weight(pieces):
    whole = jnp.concatenate(pieces, 1).astype(jnp.bfloat16)
    return lax.psum_scatter(whole, "dp", scatter_dimension=0, tiled=True).astype(jnp.float32)


def forward_product(rows, weight):
    return lax.dot_general(
        rows, weight, (((2,), (0,)), ((), ())), preferred_element_type=jnp.float32
    )


def back_product(rows, weight):
    return lax.dot_general(
        rows, weight, (((2,), (1,)), ((), ())), preferred_element_type=jnp.float32
    )


def weight_product(rows, gradient):
    return lax.dot_general(
        rows, gradient, (((0, 1), (0, 1)), ((), ())), preferred_element_type=jnp.float32
    )


def cut_columns(value, widths):
    parts, at = [], 0
    for width in widths:
        parts.append(value[..., at : at + width])
        at += width
    return parts


def on_device(
    states,
    encoder,
    upstream,
    decoder_docs,
    encoder_docs,
    norm_self,
    norm_cross,
    norm_feed,
    position_table,
    self_query,
    self_key,
    self_value,
    self_output,
    cross_query,
    cross_key,
    cross_value,
    cross_output,
    feed_gate,
    feed_up,
    feed_down,
):
    parts, _, width = states.shape
    length = decoder_docs.shape[1]
    encoder_length = encoder_docs.shape[1]
    inner = self_query.shape[1]
    hidden = feed_gate.shape[1]
    heads = inner // HEAD_DIM
    block = 256
    low = jnp.bfloat16

    self_in = gather_weight([self_query, self_key, self_value])
    middle = gather_weight([self_output.T, cross_query, cross_key, cross_value, cross_output.T])
    feed = gather_weight([feed_gate, feed_up, feed_down.T])
    self_out, query_cross, both_cross, cross_out = cut_columns(
        middle, (inner, inner, 2 * inner, inner)
    )
    feed_in, feed_out = cut_columns(feed, (2 * hidden, hidden))

    tensor_index = lax.axis_index("tensor")
    table = lax.dynamic_slice_in_dim(position_table, tensor_index * heads, heads, 1).T
    docs_column = decoder_docs[:, :, None]
    docs_row = decoder_docs[:, None, :]
    encoder_row = encoder_docs[:, None, :]

    residual = states.astype(jnp.float32)
    normed, scale_self = norm_forward(residual, norm_self)
    whole_self = gather_rows(normed)
    encoder_whole = gather_rows(encoder)
    upper = gather_rows(upstream)

    qkv = forward_product(whole_self, self_in).astype(low)
    log_shape = jax.ShapeDtypeStruct((parts, length, heads), jnp.float32)
    mixed_shape = jax.ShapeDtypeStruct((parts, length, inner), low)
    self_mixed, self_log = per_sequence(
        functools.partial(self_forward_kernel, heads, block),
        table,
        (docs_column, docs_row, qkv),
        (mixed_shape, log_shape),
    )
    residual_one = residual + scatter_rows(back_product(self_mixed, self_out))
    normed, scale_cross = norm_forward(residual_one, norm_cross)
    whole_cross = gather_rows(normed)
    both = forward_product(encoder_whole, both_cross).astype(low)
    queries = forward_product(whole_cross, query_cross).astype(low)
    cross_mixed, cross_log = per_sequence(
        functools.partial(cross_forward_kernel, heads, block),
        None,
        (docs_column, encoder_row, queries, both),
        (mixed_shape, log_shape),
    )
    residual_two = residual_one + scatter_rows(back_product(cross_mixed, cross_out))
    normed, scale_feed = norm_forward(residual_two, norm_feed)
    whole_feed = gather_rows(normed)
    gate, upward = cut_columns(forward_product(whole_feed, feed_in), (hidden, hidden))
    activated, slope = gelu_parts(gate)
    hidden_state = (activated * upward).astype(low)
    feed_result = scatter_rows(back_product(hidden_state, feed_out))
    layer_output = (residual_two + feed_result).astype(low)

    hidden_grad = forward_product(upper, feed_out)
    gate_grad = (hidden_grad * upward * slope).astype(low)
    up_grad = (hidden_grad * activated).astype(low)
    both_grad = jnp.concatenate([gate_grad, up_grad], 2)
    feed_grad = scatter_rows(back_product(both_grad, feed_in))
    feed_weights = scatter_weight(
        [weight_product(whole_feed, both_grad), weight_product(upper, hidden_state)]
    )
    step_grad, norm_feed_gradient = norm_backward(residual_two, scale_feed, norm_feed, feed_grad)
    grad_two = upstream.astype(jnp.float32) + step_grad

    upper_two = gather_rows(grad_two.astype(low))
    mixed_grad = forward_product(upper_two, cross_out).astype(low)
    query_grad, both_grad = per_sequence(
        functools.partial(cross_backward_kernel, heads, block),
        None,
        (docs_column, encoder_row, queries, both, cross_log, mixed_grad),
        (mixed_shape, jax.ShapeDtypeStruct((parts, encoder_length, 2 * inner), low)),
    )
    cross_grad = scatter_rows(back_product(query_grad, query_cross))
    encoder_gradient = scatter_rows(back_product(both_grad, both_cross))
    cross_query_whole = weight_product(whole_cross, query_grad)
    cross_both_whole = weight_product(encoder_whole, both_grad)
    cross_output_whole = weight_product(upper_two, cross_mixed)
    step_grad, norm_cross_gradient = norm_backward(residual_one, scale_cross, norm_cross, cross_grad)
    grad_one = grad_two + step_grad

    upper_one = gather_rows(grad_one.astype(low))
    self_output_whole = weight_product(upper_one, self_mixed)
    middle_weights = scatter_weight(
        [self_output_whole, cross_query_whole, cross_both_whole, cross_output_whole]
    )
    mixed_grad = forward_product(upper_one, self_out).astype(low)
    qkv_grad, diagonal = per_sequence(
        functools.partial(self_backward_kernel, heads, block),
        table,
        (docs_column, docs_row, qkv, self_log, mixed_grad),
        (
            jax.ShapeDtypeStruct((parts, length, 3 * inner), low),
            jax.ShapeDtypeStruct((parts, heads, 2 * block), jnp.float32),
        ),
    )
    normed_grad = scatter_rows(back_product(qkv_grad, self_in))
    self_weights = scatter_weight([weight_product(whole_self, qkv_grad)])
    step_grad, norm_self_gradient = norm_backward(residual, scale_self, norm_self, normed_grad)
    states_gradient = grad_one + step_grad

    count = distance_buckets(window_distance((1, 2 * block), 2 * block, block))
    onehot = (count == jnp.arange(BUCKETS, dtype=jnp.int32)[:, None]).astype(jnp.float32)
    table_local = jnp.dot(onehot, jnp.sum(diagonal, 0).T, precision=lax.Precision.HIGHEST)
    table_full = lax.dynamic_update_slice_in_dim(
        jnp.zeros(position_table.shape, jnp.float32), table_local, tensor_index * heads, 1
    )
    small = jnp.concatenate(
        [norm_self_gradient, norm_cross_gradient, norm_feed_gradient, table_full.reshape(-1)]
    )
    small = lax.psum(small, ("dp", "tensor"))

    query_self_g, key_self_g, value_self_g = cut_columns(self_weights, (inner,) * 3)
    self_out_g, query_cross_g, key_cross_g, value_cross_g, cross_out_g = cut_columns(
        middle_weights, (inner,) * 5
    )
    gate_g, up_g, down_g = cut_columns(feed_weights, (hidden,) * 3)
    return (
        layer_output,
        states_gradient,
        encoder_gradient,
        small[:width],
        small[width : 2 * width],
        small[2 * width : 3 * width],
        small[3 * width :].reshape(position_table.shape),
        query_self_g,
        key_self_g,
        value_self_g,
        self_out_g.T,
        query_cross_g,
        key_cross_g,
        value_cross_g,
        cross_out_g.T,
        gate_g,
        up_g,
        down_g.T,
    )


def solution(mesh):
    return jax.shard_map(
        on_device,
        mesh=mesh,
        in_specs=(
            P("dp", "tensor", None),
            P("dp", "tensor", None),
            P("dp", "tensor", None),
            P("dp", None),
            P("dp", None),
            P(),
            P(),
            P(),
            P(),
            P("dp", "tensor"),
            P("dp", "tensor"),
            P("dp", "tensor"),
            P("tensor", "dp"),
            P("dp", "tensor"),
            P("dp", "tensor"),
            P("dp", "tensor"),
            P("tensor", "dp"),
            P("dp", "tensor"),
            P("dp", "tensor"),
            P("tensor", "dp"),
        ),
        out_specs=(
            P("dp", "tensor", None),
            P("dp", "tensor", None),
            P("dp", "tensor", None),
            P(),
            P(),
            P(),
            P(),
            P("dp", "tensor"),
            P("dp", "tensor"),
            P("dp", "tensor"),
            P("tensor", "dp"),
            P("dp", "tensor"),
            P("dp", "tensor"),
            P("dp", "tensor"),
            P("tensor", "dp"),
            P("dp", "tensor"),
            P("dp", "tensor"),
            P("tensor", "dp"),
        ),
        check_vma=False,
    )
```

```python
import functools
import math

import jax
import jax.numpy as jnp
from jax import lax
from jax.experimental import pallas as pl
from jax.experimental.pallas import tpu as pltpu
from jax.sharding import PartitionSpec as P

HEADS = 12
HEAD_DIM = 64
BUCKETS = 32

EPS = 1e-06
NEG = -1e30
far_distance = 128


def bucket_edges():
    half = BUCKETS // 2
    upper = [
        int(math.ceil(half * (far_distance / half) ** (step / half)))
        for step in range(1, BUCKETS - half)
    ]
    return list(range(1, half + 1)) + upper


def distance_buckets(distance):
    count = jnp.zeros(distance.shape, jnp.int32)
    for edge in bucket_edges():
        count = count + (distance >= edge).astype(jnp.int32)
    return count


def dot(left, right, left_dim, right_dim):
    return lax.dot_general(
        left, right, (((left_dim,), (right_dim,)), ((), ())), preferred_element_type=jnp.float32
    )


def window_distance(shape, window, block):
    place = lax.broadcasted_iota(jnp.int32, shape, len(shape) - 1)
    return jnp.where(place > block, block + window - place, block - place)


def bias_window(table_ref, head, block):
    window = 2 * block
    distance = window_distance((8, window), window, block)
    count = distance_buckets(distance)
    line = jnp.zeros((8, window), jnp.float32)
    for bucket in range(BUCKETS):
        line = jnp.where(count == bucket, table_ref[head, bucket], line)
    row = lax.broadcasted_iota(jnp.int32, (8, window), 0)
    for step in (1, 2, 4):
        line = jnp.where((row & step) != 0, pltpu.roll(line, step, 1), line)
    step = 8
    while step < block:
        line = jnp.concatenate([line, pltpu.roll(line, step, 1)], 0)
        step = 2 * step
    return line


def diagonal_sums(tile, block):
    window = 2 * block
    step = block // 2
    while step >= 8:
        tile = tile[:step] + pltpu.roll(tile[step:], window - step, 1)
        step = step // 2
    row = lax.broadcasted_iota(jnp.int32, (8, window), 0)
    for step in (1, 2, 4):
        tile = jnp.where((row & step) != 0, pltpu.roll(tile, window - step, 1), tile)
    return jnp.sum(tile, 0, keepdims=True)


def self_scores(query, keys, docs_column, docs_row, index, block, table_ref, head, wide):
    size = (index + 1) * block
    raw = dot(query, keys[:size], 1, 1)
    parts = []
    for other in range(index + 1):
        piece = raw[:, other * block : (other + 1) * block]
        if other == index:
            piece = piece + wide[:, block:]
        elif other == index - 1:
            piece = piece + wide[:, :block]
        else:
            piece = piece + table_ref[head, BUCKETS - 1]
        same = docs_column == docs_row[:, other * block : (other + 1) * block]
        if other == index:
            place = lax.broadcasted_iota(jnp.int32, (block, block), 0)
            same = same & (place >= lax.broadcasted_iota(jnp.int32, (block, block), 1))
        parts.append(jnp.where(same, piece, NEG))
    return jnp.concatenate(parts, 1) if len(parts) > 1 else parts[0]


def softmax_mix(scores, values):
    top = jnp.max(scores, -1, keepdims=True)
    lifted = jnp.exp(scores - top)
    total = jnp.sum(lifted, -1, keepdims=True)
    shares = (lifted * (1.0 / total)).astype(jnp.bfloat16)
    return dot(shares, values, 1, 0).astype(jnp.bfloat16), top + jnp.log(total)


def head_slice(head):
    return slice(head * HEAD_DIM, (head + 1) * HEAD_DIM)


def self_forward_kernel(heads, block, table_ref, column_ref, row_ref, qkv_ref, mixed_ref, log_ref):
    width = heads * HEAD_DIM
    length = qkv_ref.shape[1]
    qkv = qkv_ref[0]
    docs_row = row_ref[0]
    mixed_heads, log_heads = [], []
    for head in range(heads):
        wide = bias_window(table_ref, head, block)
        cut = head_slice(head)
        query, keys, values = (
            qkv[:, part * width + cut.start : part * width + cut.stop] for part in range(3)
        )
        mixed_blocks, log_blocks = [], []
        for index in range(length // block):
            rows = slice(index * block, (index + 1) * block)
            scores = self_scores(
                query[rows], keys, column_ref[0, rows], docs_row, index, block, table_ref, head, wide
            )
            mixed, log_total = softmax_mix(scores, values[: rows.stop])
            mixed_blocks.append(mixed)
            log_blocks.append(log_total)
        mixed_heads.append(jnp.concatenate(mixed_blocks, 0))
        log_heads.append(jnp.concatenate(log_blocks, 0))
    mixed_ref[0] = jnp.concatenate(mixed_heads, 1)
    log_ref[0] = jnp.concatenate(log_heads, 1)


def self_backward_kernel(
    heads, block, table_ref, column_ref, row_ref, qkv_ref, log_ref, grad_ref, out_ref, diagonal_ref
):
    width = heads * HEAD_DIM
    length = qkv_ref.shape[1]
    window = 2 * block
    qkv = qkv_ref[0]
    grads = grad_ref[0]
    docs_row = row_ref[0]
    query_heads, key_heads, value_heads = [], [], []
    for head in range(heads):
        wide = bias_window(table_ref, head, block)
        cut = head_slice(head)
        query, keys, values = (
            qkv[:, part * width + cut.start : part * width + cut.stop] for part in range(3)
        )
        grad = grads[:, cut]
        blocks = length // block
        key_sums = [None] * blocks
        value_sums = [None] * blocks
        query_blocks = []
        near = jnp.zeros((block, block), jnp.float32)
        before = jnp.zeros((block, block), jnp.float32)
        far = jnp.zeros((1, block), jnp.float32)
        for index in range(blocks):
            rows = slice(index * block, (index + 1) * block)
            scores = self_scores(
                query[rows], keys, column_ref[0, rows], docs_row, index, block, table_ref, head, wide
            )
            shares = jnp.exp(scores - log_ref[0, rows, head : head + 1])
            share_grad = dot(grad[rows], values[: rows.stop], 1, 1)
            inner = jnp.sum(shares * share_grad, -1, keepdims=True)
            score_grad = shares * (share_grad - inner)
            low = score_grad.astype(jnp.bfloat16)
            query_blocks.append(dot(low, keys[: rows.stop], 1, 0).astype(jnp.bfloat16))
            key_part = dot(low, query[rows], 0, 0)
            value_part = dot(shares.astype(jnp.bfloat16), grad[rows], 0, 0)
            for other in range(index + 1):
                cols = slice(other * block, (other + 1) * block)
                key_sums[other] = (
                    key_part[cols] if key_sums[other] is None else key_sums[other] + key_part[cols]
                )
                value_sums[other] = (
                    value_part[cols]
                    if value_sums[other] is None
                    else value_sums[other] + value_part[cols]
                )
                if other == index:
                    near = near + score_grad[:, cols]
                elif other == index - 1:
                    before = before + score_grad[:, cols]
                else:
                    far = far + jnp.sum(score_grad[:, cols], 0, keepdims=True)
        line = diagonal_sums(jnp.concatenate([before, near], 1), block)
        place = lax.broadcasted_iota(jnp.int32, (1, window), 1)
        line = jnp.where(place == block + 1, line + jnp.sum(far), line)
        diagonal_ref[0, head : head + 1] = line
        query_heads.append(jnp.concatenate(query_blocks, 0))
        key_heads.append(jnp.concatenate(key_sums, 0).astype(jnp.bfloat16))
        value_heads.append(jnp.concatenate(value_sums, 0).astype(jnp.bfloat16))
    out_ref[0] = jnp.concatenate(query_heads + key_heads + value_heads, 1)


def cross_scores(query, keys, docs_column, docs_row):
    return jnp.where(docs_column == docs_row, dot(query, keys, 1, 1), NEG)


def cross_forward_kernel(heads, block, column_ref, row_ref, query_ref, both_ref, mixed_ref, log_ref):
    width = heads * HEAD_DIM
    both = both_ref[0]
    for index in range(query_ref.shape[1] // block):
        rows = slice(index * block, (index + 1) * block)
        mixed_heads, log_heads = [], []
        for head in range(heads):
            cut = head_slice(head)
            scores = cross_scores(
                query_ref[0, rows, cut], both[:, cut], column_ref[0, rows], row_ref[0]
            )
            mixed, log_total = softmax_mix(scores, both[:, width + cut.start : width + cut.stop])
            mixed_heads.append(mixed)
            log_heads.append(log_total)
        mixed_ref[0, rows] = jnp.concatenate(mixed_heads, 1)
        log_ref[0, rows] = jnp.concatenate(log_heads, 1)


def cross_backward_kernel(
    heads, block, column_ref, row_ref, query_ref, both_ref, log_ref, grad_ref, out_ref, both_out_ref
):
    width = heads * HEAD_DIM
    both = both_ref[0]
    query_heads, key_heads, value_heads = [], [], []
    for head in range(heads):
        cut = head_slice(head)
        keys = both[:, cut]
        values = both[:, width + cut.start : width + cut.stop]
        key_sum = value_sum = None
        query_blocks = []
        for index in range(query_ref.shape[1] // block):
            rows = slice(index * block, (index + 1) * block)
            query = query_ref[0, rows, cut]
            grad = grad_ref[0, rows, cut]
            scores = cross_scores(query, keys, column_ref[0, rows], row_ref[0])
            shares = jnp.exp(scores - log_ref[0, rows, head : head + 1])
            share_grad = dot(grad, values, 1, 1)
            inner = jnp.sum(shares * share_grad, -1, keepdims=True)
            low = (shares * (share_grad - inner)).astype(jnp.bfloat16)
            query_blocks.append(dot(low, keys, 1, 0).astype(jnp.bfloat16))
            key_part = dot(low, query, 0, 0)
            value_part = dot(shares.astype(jnp.bfloat16), grad, 0, 0)
            key_sum = key_part if key_sum is None else key_sum + key_part
            value_sum = value_part if value_sum is None else value_sum + value_part
        query_heads.append(jnp.concatenate(query_blocks, 0))
        key_heads.append(key_sum.astype(jnp.bfloat16))
        value_heads.append(value_sum.astype(jnp.bfloat16))
    out_ref[0] = jnp.concatenate(query_heads, 1)
    both_out_ref[0] = jnp.concatenate(key_heads + value_heads, 1)


def whole_block(value):
    shape = (1,) + value.shape[1:]
    return pl.BlockSpec(shape, lambda part: (part,) + (0,) * (len(shape) - 1))


def per_sequence(kernel, table, arrays, outs):
    ins = [whole_block(value) for value in arrays]
    operands = list(arrays)
    if table is not None:
        ins.insert(0, pl.BlockSpec(memory_space=pltpu.SMEM))
        operands.insert(0, table)
    return pl.pallas_call(
        kernel,
        grid=(arrays[0].shape[0],),
        in_specs=ins,
        out_specs=[whole_block(value) for value in outs],
        out_shape=outs,
        compiler_params=pltpu.CompilerParams(vmem_limit_bytes=56 * 1024 * 1024),
    )(*operands)


MESH = pl.DeviceIdType.MESH


def exchange_kernel(sums, extras, locals_, gathers, chunks, body, *refs):
    partial_refs = refs[:sums]
    extra_refs = refs[sums : sums + extras]
    at = sums + extras
    local_refs = refs[at : at + locals_]
    gather_refs = refs[at + locals_ : at + locals_ + gathers]
    at = at + locals_ + gathers
    near_refs = refs[at : at + sums]
    far_refs = refs[at + sums : at + 2 * sums]
    out_refs = refs[at + 2 * sums : at + 3 * sums]
    send_sem, recv_sem = refs[at + 3 * sums :]
    me = lax.axis_index("tensor")
    sibling = me + 1 - 2 * lax.rem(me, 2)
    across = lax.rem(me + 2, 4)
    diagonal = lax.rem(sibling + 2, 4)
    barrier = pltpu.get_barrier_semaphore()
    for peer in (sibling, across):
        pl.semaphore_signal(barrier, inc=1, device_id={"tensor": peer}, device_id_type=MESH)
    pl.semaphore_wait(barrier, 2)
    used = [0]

    def send(source, target, peer):
        slot = used[0]
        used[0] += 1
        copy = pltpu.make_async_remote_copy(
            src_ref=source,
            dst_ref=target,
            send_sem=send_sem.at[slot],
            recv_sem=recv_sem.at[slot],
            device_id={"tensor": peer},
            device_id_type=MESH,
        )
        copy.start()
        return copy

    sent = []
    first, second, third = [], [], []
    for which in range(sums):
        rows = partial_refs[which].shape[2] // chunks
        for chunk in range(chunks):
            cut = pl.ds(chunk * rows, rows)
            first.append(
                send(
                    partial_refs[which].at[:, diagonal, cut],
                    near_refs[which].at[1, :, cut],
                    sibling,
                )
            )
    for which in range(sums):
        rows = partial_refs[which].shape[2] // chunks
        for chunk in range(chunks):
            cut = pl.ds(chunk * rows, rows)
            second.append(
                send(
                    partial_refs[which].at[:, sibling, cut],
                    near_refs[which].at[0, :, cut],
                    sibling,
                )
            )
    for which in range(sums):
        rows = partial_refs[which].shape[2] // chunks
        for chunk in range(chunks):
            cut = pl.ds(chunk * rows, rows)
            first[which * chunks + chunk].wait_recv()
            mine = partial_refs[which][:, across, cut].astype(jnp.float32)
            theirs = near_refs[which][1, :, cut].astype(jnp.float32)
            out_refs[which][:, cut] = (mine + theirs).astype(jnp.bfloat16)
            third.append(send(out_refs[which].at[:, cut], far_refs[which].at[:, cut], across))
    totals = []
    for copy in second + third:
        copy.wait_recv()
    for which in range(sums):
        totals.append(
            partial_refs[which][:, me].astype(jnp.float32)
            + near_refs[which][0].astype(jnp.float32)
            + far_refs[which][...].astype(jnp.float32)
        )
    local_values, gather_values = body(totals, [ref[...] for ref in extra_refs])
    for ref, value in zip(local_refs, local_values):
        ref[...] = value
    over, beside, relay = [], [], []
    for ref, value in zip(gather_refs, gather_values):
        ref[:, me] = value
        count = chunks if ref.shape[2] % (16 * chunks) == 0 else 1
        rows = ref.shape[2] // count
        for chunk in range(count):
            piece = ref.at[:, me, pl.ds(chunk * rows, rows)]
            over.append((ref, pl.ds(chunk * rows, rows), send(piece, piece, across)))
    for ref in gather_refs:
        beside.append(send(ref.at[:, me], ref.at[:, me], sibling))
    for ref, cut, copy in over:
        copy.wait_recv()
        piece = ref.at[:, across, cut]
        relay.append(send(piece, piece, sibling))
    for copy in beside + relay:
        copy.wait_recv()
    for copy in first + second + third + beside + relay + [item[2] for item in over]:
        copy.wait_send()


def exchange(collective, body, partials, extras, locals_, gathers, chunks=2):
    split = [
        value.reshape(value.shape[0], 4, value.shape[1] // 4, value.shape[2]) for value in partials
    ]
    blocks = [(value.shape[0],) + value.shape[2:] for value in split]
    low = jnp.bfloat16
    scratch = [pltpu.VMEM((2,) + block, low) for block in blocks]
    scratch += [pltpu.VMEM(block, low) for block in blocks + blocks]
    copies = 3 * chunks * len(split) + (2 * chunks + 1) * len(gathers)
    scratch += [pltpu.SemaphoreType.DMA((copies,)), pltpu.SemaphoreType.DMA((copies,))]
    shapes = list(locals_) + [
        jax.ShapeDtypeStruct((value.shape[0], 4) + value.shape[1:], value.dtype)
        for value in gathers
    ]
    results = pl.pallas_call(
        functools.partial(
            exchange_kernel, len(split), len(extras), len(locals_), len(gathers), chunks, body
        ),
        in_specs=[pl.BlockSpec(memory_space=pltpu.VMEM)] * (len(split) + len(extras)),
        out_specs=[pl.BlockSpec(memory_space=pltpu.VMEM)] * len(shapes),
        out_shape=shapes,
        scratch_shapes=scratch,
        compiler_params=pltpu.CompilerParams(
            collective_id=collective, has_side_effects=True, vmem_limit_bytes=48 * 1024 * 1024
        ),
    )(*split, *extras)
    local_results = list(results[: len(locals_)])
    whole = [
        value.reshape(value.shape[0], 4 * value.shape[2], value.shape[3])
        for value in results[len(locals_) :]
    ]
    return local_results + whole


def spread_kernel(count, big_ref, small_ref, big_out, small_out, slots, small_slots, *sems):
    big_send, big_recv, small_send, small_recv = sems
    me = lax.axis_index("dp")
    barrier = pltpu.get_barrier_semaphore()
    for step in range(1, count):
        peer = lax.rem(me + step, count)
        pl.semaphore_signal(barrier, inc=1, device_id={"dp": peer}, device_id_type=MESH)
    pl.semaphore_wait(barrier, count - 1)
    copies = []
    for step in range(1, count):
        peer = lax.rem(me + step, count)
        for source, target, send_sem, recv_sem in (
            (big_ref.at[peer], slots.at[step - 1], big_send, big_recv),
            (small_ref, small_slots.at[step - 1], small_send, small_recv),
        ):
            copy = pltpu.make_async_remote_copy(
                src_ref=source,
                dst_ref=target,
                send_sem=send_sem.at[step - 1],
                recv_sem=recv_sem.at[step - 1],
                device_id={"dp": peer},
                device_id_type=MESH,
            )
            copy.start()
            copies.append(copy)
    big_out[...] = big_ref[me].astype(jnp.float32)
    small_out[...] = small_ref[...]
    for step in range(1, count):
        copies[2 * step - 2].wait_recv()
        big_out[...] += slots[step - 1].astype(jnp.float32)
        copies[2 * step - 1].wait_recv()
    small_out[...] = small_ref[...] + jnp.sum(small_slots[...], 0)
    for copy in copies:
        copy.wait_send()


def spread_sum(collective, count, big, small):
    big = big.reshape(count, big.shape[0] // count, big.shape[1])
    return pl.pallas_call(
        functools.partial(spread_kernel, count),
        in_specs=[pl.BlockSpec(memory_space=pltpu.VMEM)] * 2,
        out_specs=[pl.BlockSpec(memory_space=pltpu.VMEM)] * 2,
        out_shape=[
            jax.ShapeDtypeStruct(big.shape[1:], jnp.float32),
            jax.ShapeDtypeStruct(small.shape, jnp.float32),
        ],
        scratch_shapes=[
            pltpu.VMEM((count - 1,) + big.shape[1:], big.dtype),
            pltpu.VMEM((count - 1,) + small.shape, small.dtype),
        ]
        + [pltpu.SemaphoreType.DMA((count - 1,))] * 4,
        compiler_params=pltpu.CompilerParams(
            collective_id=collective, has_side_effects=True, vmem_limit_bytes=48 * 1024 * 1024
        ),
    )(big, small)


def norm_forward(rows, gain):
    scale = lax.rsqrt(jnp.mean(rows * rows, -1, keepdims=True) + EPS)
    return (rows * scale * gain).astype(jnp.bfloat16), scale


def norm_backward(rows, scale, gain, normed_grad):
    unit = rows * scale
    inward = normed_grad * gain
    rows_grad = scale * (inward - unit * jnp.mean(inward * unit, -1, keepdims=True))
    gain_grad = jnp.sum(jnp.sum(normed_grad * unit, 0, keepdims=True), 1, keepdims=True)
    return rows_grad, gain_grad


def gelu_parts(value):
    inner = math.sqrt(2 / math.pi) * (value + 0.044715 * value * value * value)
    curve = jnp.tanh(inner)
    activated = 0.5 * value * (1 + curve)
    slope = 0.5 * (1 + curve) + 0.5 * value * (1 - curve * curve) * math.sqrt(2 / math.pi) * (
        1 + 3 * 0.044715 * value * value
    )
    return activated, slope


def sum_body(totals, extras):
    return totals, []


def start_body(totals, extras):
    states, encoder, upstream, gain = extras
    normed, scale = norm_forward(states.astype(jnp.float32), gain)
    return [scale], [normed, encoder, upstream]


def forward_body(totals, extras):
    before, gain = extras
    rows = before + totals[0]
    normed, scale = norm_forward(rows, gain)
    return [rows, scale], [normed]


def backward_body(totals, extras):
    rows, scale, gain, upper = extras[:4]
    step_grad, gain_grad = norm_backward(rows, scale, gain, totals[0])
    rows_grad = upper.astype(jnp.float32) + step_grad
    return [rows_grad, gain_grad] + totals[1:], [rows_grad.astype(jnp.bfloat16)]


def last_body(totals, extras):
    states, scale, gain, upper, small = extras
    rows = states.astype(jnp.float32)
    step_grad, gain_grad = norm_backward(rows, scale, gain, totals[0])
    place = lax.broadcasted_iota(jnp.int32, small.shape, 1)
    return [upper + step_grad], [jnp.where(place == 0, gain_grad, small)]


def gather_weight(pieces):
    return lax.all_gather(jnp.concatenate(pieces, 1), "dp", axis=0, tiled=True)


def scatter_weight(pieces):
    whole = jnp.concatenate(pieces, 1).astype(jnp.bfloat16)
    return lax.psum_scatter(whole, "dp", scatter_dimension=0, tiled=True).astype(jnp.float32)


def forward_product(rows, weight):
    return lax.dot_general(
        rows, weight, (((2,), (0,)), ((), ())), preferred_element_type=jnp.float32
    )


def back_product(rows, weight):
    return lax.dot_general(
        rows, weight, (((2,), (1,)), ((), ())), preferred_element_type=jnp.float32
    )


def weight_product(rows, gradient):
    return lax.dot_general(
        rows, gradient, (((0, 1), (0, 1)), ((), ())), preferred_element_type=jnp.float32
    )


def cut_columns(value, widths):
    parts, at = [], 0
    for width in widths:
        parts.append(value[..., at : at + width])
        at += width
    return parts


def on_device(
    states,
    encoder,
    upstream,
    decoder_docs,
    encoder_docs,
    norm_self,
    norm_cross,
    norm_feed,
    position_table,
    self_query,
    self_key,
    self_value,
    self_output,
    cross_query,
    cross_key,
    cross_value,
    cross_output,
    feed_gate,
    feed_up,
    feed_down,
):
    parts, _, width = states.shape
    length = decoder_docs.shape[1]
    encoder_length = encoder_docs.shape[1]
    inner = self_query.shape[1]
    hidden = feed_gate.shape[1]
    heads = inner // HEAD_DIM
    block = 256
    low = jnp.bfloat16

    self_in = gather_weight([self_query, self_key, self_value])
    middle = gather_weight([self_output.T, cross_query, cross_key, cross_value, cross_output.T])
    feed = gather_weight([feed_gate, feed_up, feed_down.T])
    self_out, query_cross, both_cross, cross_out = cut_columns(
        middle, (inner, inner, 2 * inner, inner)
    )
    feed_in, feed_out = cut_columns(feed, (2 * hidden, hidden))

    tensor_index = lax.axis_index("tensor")
    table = lax.dynamic_slice_in_dim(position_table, tensor_index * heads, heads, 1).T
    docs_column = decoder_docs[:, :, None]
    docs_row = decoder_docs[:, None, :]
    encoder_row = encoder_docs[:, None, :]

    residual = states.astype(jnp.float32)
    rows_shape = jax.ShapeDtypeStruct(states.shape, jnp.float32)
    encoder_shape = jax.ShapeDtypeStruct(encoder.shape, jnp.float32)
    scale_shape = jax.ShapeDtypeStruct(states.shape[:2] + (1,), jnp.float32)
    gain_shape = jax.ShapeDtypeStruct((1, 1, width), jnp.float32)
    gain_self, gain_cross, gain_feed = (
        gain.reshape(1, 1, width) for gain in (norm_self, norm_cross, norm_feed)
    )
    scale_self, whole_self, encoder_whole, upper = exchange(
        0,
        start_body,
        [],
        [states, encoder, upstream, gain_self],
        [scale_shape],
        [states, encoder, upstream],
    )

    qkv = forward_product(whole_self, self_in).astype(low)
    log_shape = jax.ShapeDtypeStruct((parts, length, heads), jnp.float32)
    mixed_shape = jax.ShapeDtypeStruct((parts, length, inner), low)
    self_mixed, self_log = per_sequence(
        functools.partial(self_forward_kernel, heads, block),
        table,
        (docs_column, docs_row, qkv),
        (mixed_shape, log_shape),
    )
    residual_one, scale_cross, whole_cross = exchange(
        1,
        forward_body,
        [back_product(self_mixed, self_out).astype(low)],
        [residual, gain_cross],
        [rows_shape, scale_shape],
        [states],
    )
    both = forward_product(encoder_whole, both_cross).astype(low)
    queries = forward_product(whole_cross, query_cross).astype(low)
    cross_mixed, cross_log = per_sequence(
        functools.partial(cross_forward_kernel, heads, block),
        None,
        (docs_column, encoder_row, queries, both),
        (mixed_shape, log_shape),
    )
    residual_two, scale_feed, whole_feed = exchange(
        2,
        forward_body,
        [back_product(cross_mixed, cross_out).astype(low)],
        [residual_one, gain_feed],
        [rows_shape, scale_shape],
        [states],
    )
    gate, upward = cut_columns(forward_product(whole_feed, feed_in), (hidden, hidden))
    activated, slope = gelu_parts(gate)
    hidden_state = (activated * upward).astype(low)
    feed_result = back_product(hidden_state, feed_out).astype(low)

    hidden_grad = forward_product(upper, feed_out)
    gate_grad = (hidden_grad * upward * slope).astype(low)
    up_grad = (hidden_grad * activated).astype(low)
    both_grad = jnp.concatenate([gate_grad, up_grad], 2)
    feed_weights = scatter_weight(
        [weight_product(whole_feed, both_grad), weight_product(upper, hidden_state)]
    )
    grad_two, norm_feed_gradient, feed_total, upper_two = exchange(
        3,
        backward_body,
        [back_product(both_grad, feed_in).astype(low), feed_result],
        [residual_two, scale_feed, gain_feed, upstream],
        [rows_shape, gain_shape, rows_shape],
        [states],
    )
    layer_output = (residual_two + feed_total).astype(low)

    mixed_grad = forward_product(upper_two, cross_out).astype(low)
    query_grad, both_grad = per_sequence(
        functools.partial(cross_backward_kernel, heads, block),
        None,
        (docs_column, encoder_row, queries, both, cross_log, mixed_grad),
        (mixed_shape, jax.ShapeDtypeStruct((parts, encoder_length, 2 * inner), low)),
    )
    cross_query_whole = weight_product(whole_cross, query_grad)
    cross_both_whole = weight_product(encoder_whole, both_grad)
    cross_output_whole = weight_product(upper_two, cross_mixed)
    grad_one, norm_cross_gradient, encoder_total, upper_one = exchange(
        4,
        backward_body,
        [
            back_product(query_grad, query_cross).astype(low),
            back_product(both_grad, both_cross).astype(low),
        ],
        [residual_one, scale_cross, gain_cross, grad_two],
        [rows_shape, gain_shape, encoder_shape],
        [states],
    )
    encoder_gradient = encoder_total + 0.0
    self_output_whole = weight_product(upper_one, self_mixed)
    mixed_grad = forward_product(upper_one, self_out).astype(low)
    qkv_grad, diagonal = per_sequence(
        functools.partial(self_backward_kernel, heads, block),
        table,
        (docs_column, docs_row, qkv, self_log, mixed_grad),
        (
            jax.ShapeDtypeStruct((parts, length, 3 * inner), low),
            jax.ShapeDtypeStruct((parts, heads, 2 * block), jnp.float32),
        ),
    )
    count = distance_buckets(window_distance((1, 2 * block), 2 * block, block))
    onehot = (count == jnp.arange(BUCKETS, dtype=jnp.int32)[:, None]).astype(jnp.float32)
    table_local = jnp.dot(onehot, jnp.sum(diagonal, 0).T, precision=lax.Precision.HIGHEST)
    table_full = lax.dynamic_update_slice_in_dim(
        jnp.zeros(position_table.shape, jnp.float32), table_local, tensor_index * heads, 1
    )
    table_flat = table_full.reshape(1, 1, -1)
    table_row = jnp.pad(table_flat, ((0, 0), (0, 0), (0, width - table_flat.shape[2])))
    small = jnp.concatenate(
        [
            jnp.zeros((1, 1, width), jnp.float32),
            norm_cross_gradient,
            norm_feed_gradient,
            table_row,
            jnp.zeros((1, 4, width), jnp.float32),
        ],
        1,
    )
    states_gradient, small = exchange(
        5,
        last_body,
        [back_product(qkv_grad, self_in).astype(low)],
        [states, scale_self, gain_self, grad_one, small],
        [rows_shape],
        [small],
    )
    small = jnp.sum(small.reshape(4, 8, width), 0)
    rest = jnp.concatenate(
        [
            self_output_whole,
            cross_query_whole,
            cross_both_whole,
            cross_output_whole,
            weight_product(whole_self, qkv_grad),
        ],
        1,
    ).astype(low)
    rest, small = spread_sum(6, width // self_query.shape[0], rest, small)
    middle_weights, self_weights = rest[:, : 5 * inner], rest[:, 5 * inner :]

    query_self_g, key_self_g, value_self_g = cut_columns(self_weights, (inner,) * 3)
    self_out_g, query_cross_g, key_cross_g, value_cross_g, cross_out_g = cut_columns(
        middle_weights, (inner,) * 5
    )
    gate_g, up_g, down_g = cut_columns(feed_weights, (hidden,) * 3)
    return (
        layer_output,
        states_gradient,
        encoder_gradient,
        small[0],
        small[1],
        small[2],
        small[3, : position_table.size].reshape(position_table.shape),
        query_self_g,
        key_self_g,
        value_self_g,
        self_out_g.T,
        query_cross_g,
        key_cross_g,
        value_cross_g,
        cross_out_g.T,
        gate_g,
        up_g,
        down_g.T,
    )


def solution(mesh):
    return jax.shard_map(
        on_device,
        mesh=mesh,
        in_specs=(
            P("dp", "tensor", None),
            P("dp", "tensor", None),
            P("dp", "tensor", None),
            P("dp", None),
            P("dp", None),
            P(),
            P(),
            P(),
            P(),
            P("dp", "tensor"),
            P("dp", "tensor"),
            P("dp", "tensor"),
            P("tensor", "dp"),
            P("dp", "tensor"),
            P("dp", "tensor"),
            P("dp", "tensor"),
            P("tensor", "dp"),
            P("dp", "tensor"),
            P("dp", "tensor"),
            P("tensor", "dp"),
        ),
        out_specs=(
            P("dp", "tensor", None),
            P("dp", "tensor", None),
            P("dp", "tensor", None),
            P(),
            P(),
            P(),
            P(),
            P("dp", "tensor"),
            P("dp", "tensor"),
            P("dp", "tensor"),
            P("tensor", "dp"),
            P("dp", "tensor"),
            P("dp", "tensor"),
            P("dp", "tensor"),
            P("tensor", "dp"),
            P("dp", "tensor"),
            P("dp", "tensor"),
            P("tensor", "dp"),
        ),
        check_vma=False,
    )
```

```python
import functools
import math

import jax
import jax.numpy as jnp
from jax import lax
from jax.experimental import pallas as pl
from jax.experimental.pallas import tpu as pltpu
from jax.sharding import PartitionSpec as P

HEADS = 12
HEAD_DIM = 64
BUCKETS = 32

EPS = 1e-06
NEG = -1e30
far_distance = 128


def bucket_edges():
    half = BUCKETS // 2
    upper = [
        int(math.ceil(half * (far_distance / half) ** (step / half)))
        for step in range(1, BUCKETS - half)
    ]
    return list(range(1, half + 1)) + upper


def distance_buckets(distance):
    count = jnp.zeros(distance.shape, jnp.int32)
    for edge in bucket_edges():
        count = count + (distance >= edge).astype(jnp.int32)
    return count


def dot(left, right, left_dim, right_dim):
    return lax.dot_general(
        left, right, (((left_dim,), (right_dim,)), ((), ())), preferred_element_type=jnp.float32
    )


def window_distance(shape, window, block):
    place = lax.broadcasted_iota(jnp.int32, shape, len(shape) - 1)
    return jnp.where(place > block, block + window - place, block - place)


def bias_window(table_ref, head, block):
    window = 2 * block
    distance = window_distance((8, window), window, block)
    count = distance_buckets(distance)
    line = jnp.zeros((8, window), jnp.float32)
    for bucket in range(BUCKETS):
        line = jnp.where(count == bucket, table_ref[head, bucket], line)
    row = lax.broadcasted_iota(jnp.int32, (8, window), 0)
    for step in (1, 2, 4):
        line = jnp.where((row & step) != 0, pltpu.roll(line, step, 1), line)
    step = 8
    while step < block:
        line = jnp.concatenate([line, pltpu.roll(line, step, 1)], 0)
        step = 2 * step
    return line


def diagonal_sums(tile, block):
    window = 2 * block
    step = block // 2
    while step >= 8:
        tile = tile[:step] + pltpu.roll(tile[step:], window - step, 1)
        step = step // 2
    row = lax.broadcasted_iota(jnp.int32, (8, window), 0)
    for step in (1, 2, 4):
        tile = jnp.where((row & step) != 0, pltpu.roll(tile, window - step, 1), tile)
    return jnp.sum(tile, 0, keepdims=True)


def self_scores(query, keys, docs_column, docs_row, index, block, table_ref, head, wide):
    size = (index + 1) * block
    raw = dot(query, keys[:size], 1, 1)
    parts = []
    for other in range(index + 1):
        piece = raw[:, other * block : (other + 1) * block]
        if other == index:
            piece = piece + wide[:, block:]
        elif other == index - 1:
            piece = piece + wide[:, :block]
        else:
            piece = piece + table_ref[head, BUCKETS - 1]
        same = docs_column == docs_row[:, other * block : (other + 1) * block]
        if other == index:
            place = lax.broadcasted_iota(jnp.int32, (block, block), 0)
            same = same & (place >= lax.broadcasted_iota(jnp.int32, (block, block), 1))
        parts.append(jnp.where(same, piece, NEG))
    return jnp.concatenate(parts, 1) if len(parts) > 1 else parts[0]


def softmax_mix(scores, values):
    top = jnp.max(scores, -1, keepdims=True)
    lifted = jnp.exp(scores - top)
    total = jnp.sum(lifted, -1, keepdims=True)
    shares = (lifted * (1.0 / total)).astype(jnp.bfloat16)
    return dot(shares, values, 1, 0).astype(jnp.bfloat16), top + jnp.log(total)


def head_slice(head):
    return slice(head * HEAD_DIM, (head + 1) * HEAD_DIM)


def self_forward_kernel(heads, block, table_ref, column_ref, row_ref, qkv_ref, mixed_ref, log_ref):
    width = heads * HEAD_DIM
    length = qkv_ref.shape[1]
    qkv = qkv_ref[0]
    docs_row = row_ref[0]
    mixed_heads, log_heads = [], []
    for head in range(heads):
        wide = bias_window(table_ref, head, block)
        cut = head_slice(head)
        query, keys, values = (
            qkv[:, part * width + cut.start : part * width + cut.stop] for part in range(3)
        )
        mixed_blocks, log_blocks = [], []
        for index in range(length // block):
            rows = slice(index * block, (index + 1) * block)
            scores = self_scores(
                query[rows], keys, column_ref[0, rows], docs_row, index, block, table_ref, head, wide
            )
            mixed, log_total = softmax_mix(scores, values[: rows.stop])
            mixed_blocks.append(mixed)
            log_blocks.append(log_total)
        mixed_heads.append(jnp.concatenate(mixed_blocks, 0))
        log_heads.append(jnp.concatenate(log_blocks, 0))
    mixed_ref[0] = jnp.concatenate(mixed_heads, 1)
    log_ref[0] = jnp.concatenate(log_heads, 1)


def self_backward_kernel(
    heads, block, table_ref, column_ref, row_ref, qkv_ref, log_ref, grad_ref, out_ref, diagonal_ref
):
    width = heads * HEAD_DIM
    length = qkv_ref.shape[1]
    window = 2 * block
    qkv = qkv_ref[0]
    grads = grad_ref[0]
    docs_row = row_ref[0]
    query_heads, key_heads, value_heads = [], [], []
    for head in range(heads):
        wide = bias_window(table_ref, head, block)
        cut = head_slice(head)
        query, keys, values = (
            qkv[:, part * width + cut.start : part * width + cut.stop] for part in range(3)
        )
        grad = grads[:, cut]
        blocks = length // block
        key_sums = [None] * blocks
        value_sums = [None] * blocks
        query_blocks = []
        near = jnp.zeros((block, block), jnp.float32)
        before = jnp.zeros((block, block), jnp.float32)
        far = jnp.zeros((1, block), jnp.float32)
        for index in range(blocks):
            rows = slice(index * block, (index + 1) * block)
            scores = self_scores(
                query[rows], keys, column_ref[0, rows], docs_row, index, block, table_ref, head, wide
            )
            shares = jnp.exp(scores - log_ref[0, rows, head : head + 1])
            share_grad = dot(grad[rows], values[: rows.stop], 1, 1)
            inner = jnp.sum(shares * share_grad, -1, keepdims=True)
            score_grad = shares * (share_grad - inner)
            low = score_grad.astype(jnp.bfloat16)
            query_blocks.append(dot(low, keys[: rows.stop], 1, 0).astype(jnp.bfloat16))
            key_part = dot(low, query[rows], 0, 0)
            value_part = dot(shares.astype(jnp.bfloat16), grad[rows], 0, 0)
            for other in range(index + 1):
                cols = slice(other * block, (other + 1) * block)
                key_sums[other] = (
                    key_part[cols] if key_sums[other] is None else key_sums[other] + key_part[cols]
                )
                value_sums[other] = (
                    value_part[cols]
                    if value_sums[other] is None
                    else value_sums[other] + value_part[cols]
                )
                if other == index:
                    near = near + score_grad[:, cols]
                elif other == index - 1:
                    before = before + score_grad[:, cols]
                else:
                    far = far + jnp.sum(score_grad[:, cols], 0, keepdims=True)
        line = diagonal_sums(jnp.concatenate([before, near], 1), block)
        place = lax.broadcasted_iota(jnp.int32, (1, window), 1)
        line = jnp.where(place == block + 1, line + jnp.sum(far), line)
        diagonal_ref[0, head : head + 1] = line
        query_heads.append(jnp.concatenate(query_blocks, 0))
        key_heads.append(jnp.concatenate(key_sums, 0).astype(jnp.bfloat16))
        value_heads.append(jnp.concatenate(value_sums, 0).astype(jnp.bfloat16))
    out_ref[0] = jnp.concatenate(query_heads + key_heads + value_heads, 1)


def cross_scores(query, keys, docs_column, docs_row):
    return jnp.where(docs_column == docs_row, dot(query, keys, 1, 1), NEG)


def cross_forward_kernel(heads, block, column_ref, row_ref, query_ref, both_ref, mixed_ref, log_ref):
    width = heads * HEAD_DIM
    both = both_ref[0]
    for index in range(query_ref.shape[1] // block):
        rows = slice(index * block, (index + 1) * block)
        mixed_heads, log_heads = [], []
        for head in range(heads):
            cut = head_slice(head)
            scores = cross_scores(
                query_ref[0, rows, cut], both[:, cut], column_ref[0, rows], row_ref[0]
            )
            mixed, log_total = softmax_mix(scores, both[:, width + cut.start : width + cut.stop])
            mixed_heads.append(mixed)
            log_heads.append(log_total)
        mixed_ref[0, rows] = jnp.concatenate(mixed_heads, 1)
        log_ref[0, rows] = jnp.concatenate(log_heads, 1)


def cross_backward_kernel(
    heads, block, column_ref, row_ref, query_ref, both_ref, log_ref, grad_ref, out_ref, both_out_ref
):
    width = heads * HEAD_DIM
    both = both_ref[0]
    query_heads, key_heads, value_heads = [], [], []
    for head in range(heads):
        cut = head_slice(head)
        keys = both[:, cut]
        values = both[:, width + cut.start : width + cut.stop]
        key_sum = value_sum = None
        query_blocks = []
        for index in range(query_ref.shape[1] // block):
            rows = slice(index * block, (index + 1) * block)
            query = query_ref[0, rows, cut]
            grad = grad_ref[0, rows, cut]
            scores = cross_scores(query, keys, column_ref[0, rows], row_ref[0])
            shares = jnp.exp(scores - log_ref[0, rows, head : head + 1])
            share_grad = dot(grad, values, 1, 1)
            inner = jnp.sum(shares * share_grad, -1, keepdims=True)
            low = (shares * (share_grad - inner)).astype(jnp.bfloat16)
            query_blocks.append(dot(low, keys, 1, 0).astype(jnp.bfloat16))
            key_part = dot(low, query, 0, 0)
            value_part = dot(shares.astype(jnp.bfloat16), grad, 0, 0)
            key_sum = key_part if key_sum is None else key_sum + key_part
            value_sum = value_part if value_sum is None else value_sum + value_part
        query_heads.append(jnp.concatenate(query_blocks, 0))
        key_heads.append(key_sum.astype(jnp.bfloat16))
        value_heads.append(value_sum.astype(jnp.bfloat16))
    out_ref[0] = jnp.concatenate(query_heads, 1)
    both_out_ref[0] = jnp.concatenate(key_heads + value_heads, 1)


def whole_block(value):
    shape = (1,) + value.shape[1:]
    return pl.BlockSpec(shape, lambda part: (part,) + (0,) * (len(shape) - 1))


def per_sequence(kernel, table, arrays, outs):
    ins = [whole_block(value) for value in arrays]
    operands = list(arrays)
    if table is not None:
        ins.insert(0, pl.BlockSpec(memory_space=pltpu.SMEM))
        operands.insert(0, table)
    return pl.pallas_call(
        kernel,
        grid=(arrays[0].shape[0],),
        in_specs=ins,
        out_specs=[whole_block(value) for value in outs],
        out_shape=outs,
        compiler_params=pltpu.CompilerParams(vmem_limit_bytes=56 * 1024 * 1024),
    )(*operands)


MESH = pl.DeviceIdType.MESH


def exchange_kernel(sums, extras, locals_, gathers, chunks, body, *refs):
    partial_refs = refs[:sums]
    extra_refs = refs[sums : sums + extras]
    at = sums + extras
    local_refs = refs[at : at + locals_]
    gather_refs = refs[at + locals_ : at + locals_ + gathers]
    at = at + locals_ + gathers
    near_refs = refs[at : at + sums]
    far_refs = refs[at + sums : at + 2 * sums]
    out_refs = refs[at + 2 * sums : at + 3 * sums]
    send_sem, recv_sem = refs[at + 3 * sums :]
    me = lax.axis_index("tensor")
    sibling = me + 1 - 2 * lax.rem(me, 2)
    across = lax.rem(me + 2, 4)
    diagonal = lax.rem(sibling + 2, 4)
    barrier = pltpu.get_barrier_semaphore()
    for peer in (sibling, across):
        pl.semaphore_signal(barrier, inc=1, device_id={"tensor": peer}, device_id_type=MESH)
    pl.semaphore_wait(barrier, 2)
    used = [0]

    def send(source, target, peer):
        slot = used[0]
        used[0] += 1
        copy = pltpu.make_async_remote_copy(
            src_ref=source,
            dst_ref=target,
            send_sem=send_sem.at[slot],
            recv_sem=recv_sem.at[slot],
            device_id={"tensor": peer},
            device_id_type=MESH,
        )
        copy.start()
        return copy

    sent = []
    first, second, third = [], [], []
    for which in range(sums):
        rows = partial_refs[which].shape[2] // chunks
        for chunk in range(chunks):
            cut = pl.ds(chunk * rows, rows)
            first.append(
                send(
                    partial_refs[which].at[:, diagonal, cut],
                    near_refs[which].at[1, :, cut],
                    sibling,
                )
            )
    for which in range(sums):
        rows = partial_refs[which].shape[2] // chunks
        for chunk in range(chunks):
            cut = pl.ds(chunk * rows, rows)
            second.append(
                send(
                    partial_refs[which].at[:, sibling, cut],
                    near_refs[which].at[0, :, cut],
                    sibling,
                )
            )
    for which in range(sums):
        rows = partial_refs[which].shape[2] // chunks
        for chunk in range(chunks):
            cut = pl.ds(chunk * rows, rows)
            first[which * chunks + chunk].wait_recv()
            mine = partial_refs[which][:, across, cut].astype(jnp.float32)
            theirs = near_refs[which][1, :, cut].astype(jnp.float32)
            out_refs[which][:, cut] = (mine + theirs).astype(jnp.bfloat16)
            third.append(send(out_refs[which].at[:, cut], far_refs[which].at[:, cut], across))
    totals = []
    for copy in second + third:
        copy.wait_recv()
    for which in range(sums):
        totals.append(
            partial_refs[which][:, me].astype(jnp.float32)
            + near_refs[which][0].astype(jnp.float32)
            + far_refs[which][...].astype(jnp.float32)
        )
    local_values, gather_values = body(totals, [ref[...] for ref in extra_refs])
    for ref, value in zip(local_refs, local_values):
        ref[...] = value
    over, beside, relay = [], [], []
    for ref, value in zip(gather_refs, gather_values):
        ref[:, me] = value
        count = chunks if ref.shape[2] % (16 * chunks) == 0 else 1
        rows = ref.shape[2] // count
        for chunk in range(count):
            piece = ref.at[:, me, pl.ds(chunk * rows, rows)]
            over.append((ref, pl.ds(chunk * rows, rows), send(piece, piece, across)))
    for ref in gather_refs:
        beside.append(send(ref.at[:, me], ref.at[:, me], sibling))
    for ref, cut, copy in over:
        copy.wait_recv()
        piece = ref.at[:, across, cut]
        relay.append(send(piece, piece, sibling))
    for copy in beside + relay:
        copy.wait_recv()
    for copy in first + second + third + beside + relay + [item[2] for item in over]:
        copy.wait_send()


def exchange(collective, body, partials, extras, locals_, gathers, chunks=2):
    split = [
        value.reshape(value.shape[0], 4, value.shape[1] // 4, value.shape[2]) for value in partials
    ]
    blocks = [(value.shape[0],) + value.shape[2:] for value in split]
    low = jnp.bfloat16
    scratch = [pltpu.VMEM((2,) + block, low) for block in blocks]
    scratch += [pltpu.VMEM(block, low) for block in blocks + blocks]
    copies = 3 * chunks * len(split) + (2 * chunks + 1) * len(gathers)
    scratch += [pltpu.SemaphoreType.DMA((copies,)), pltpu.SemaphoreType.DMA((copies,))]
    shapes = list(locals_) + [
        jax.ShapeDtypeStruct((value.shape[0], 4) + value.shape[1:], value.dtype)
        for value in gathers
    ]
    results = pl.pallas_call(
        functools.partial(
            exchange_kernel, len(split), len(extras), len(locals_), len(gathers), chunks, body
        ),
        in_specs=[pl.BlockSpec(memory_space=pltpu.VMEM)] * (len(split) + len(extras)),
        out_specs=[pl.BlockSpec(memory_space=pltpu.VMEM)] * len(shapes),
        out_shape=shapes,
        scratch_shapes=scratch,
        compiler_params=pltpu.CompilerParams(
            collective_id=collective, has_side_effects=True, vmem_limit_bytes=48 * 1024 * 1024
        ),
    )(*split, *extras)
    local_results = list(results[: len(locals_)])
    whole = [
        value.reshape(value.shape[0], 4 * value.shape[2], value.shape[3])
        for value in results[len(locals_) :]
    ]
    return local_results + whole


def spread_kernel(count, big_ref, small_ref, big_out, small_out, slots, small_slots, *sems):
    big_send, big_recv, small_send, small_recv = sems
    me = lax.axis_index("dp")
    barrier = pltpu.get_barrier_semaphore()
    for step in range(1, count):
        peer = lax.rem(me + step, count)
        pl.semaphore_signal(barrier, inc=1, device_id={"dp": peer}, device_id_type=MESH)
    pl.semaphore_wait(barrier, count - 1)
    copies = []
    for step in range(1, count):
        peer = lax.rem(me + step, count)
        for source, target, send_sem, recv_sem in (
            (big_ref.at[peer], slots.at[step - 1], big_send, big_recv),
            (small_ref, small_slots.at[step - 1], small_send, small_recv),
        ):
            copy = pltpu.make_async_remote_copy(
                src_ref=source,
                dst_ref=target,
                send_sem=send_sem.at[step - 1],
                recv_sem=recv_sem.at[step - 1],
                device_id={"dp": peer},
                device_id_type=MESH,
            )
            copy.start()
            copies.append(copy)
    big_out[...] = big_ref[me].astype(jnp.float32)
    small_out[...] = small_ref[...]
    for step in range(1, count):
        copies[2 * step - 2].wait_recv()
        big_out[...] += slots[step - 1].astype(jnp.float32)
        copies[2 * step - 1].wait_recv()
    small_out[...] = small_ref[...] + jnp.sum(small_slots[...], 0)
    for copy in copies:
        copy.wait_send()


def spread_sum(collective, count, big, small):
    big = big.reshape(count, big.shape[0] // count, big.shape[1])
    return pl.pallas_call(
        functools.partial(spread_kernel, count),
        in_specs=[pl.BlockSpec(memory_space=pltpu.VMEM)] * 2,
        out_specs=[pl.BlockSpec(memory_space=pltpu.VMEM)] * 2,
        out_shape=[
            jax.ShapeDtypeStruct(big.shape[1:], jnp.float32),
            jax.ShapeDtypeStruct(small.shape, jnp.float32),
        ],
        scratch_shapes=[
            pltpu.VMEM((count - 1,) + big.shape[1:], big.dtype),
            pltpu.VMEM((count - 1,) + small.shape, small.dtype),
        ]
        + [pltpu.SemaphoreType.DMA((count - 1,))] * 4,
        compiler_params=pltpu.CompilerParams(
            collective_id=collective, has_side_effects=True, vmem_limit_bytes=48 * 1024 * 1024
        ),
    )(big, small)


def norm_forward(rows, gain):
    scale = lax.rsqrt(jnp.mean(rows * rows, -1, keepdims=True) + EPS)
    return (rows * scale * gain).astype(jnp.bfloat16), scale


def norm_backward(rows, scale, gain, normed_grad):
    unit = rows * scale
    inward = normed_grad * gain
    rows_grad = scale * (inward - unit * jnp.mean(inward * unit, -1, keepdims=True))
    gain_grad = jnp.sum(jnp.sum(normed_grad * unit, 0, keepdims=True), 1, keepdims=True)
    return rows_grad, gain_grad


def gelu_parts(value):
    inner = math.sqrt(2 / math.pi) * (value + 0.044715 * value * value * value)
    curve = jnp.tanh(inner)
    activated = 0.5 * value * (1 + curve)
    slope = 0.5 * (1 + curve) + 0.5 * value * (1 - curve * curve) * math.sqrt(2 / math.pi) * (
        1 + 3 * 0.044715 * value * value
    )
    return activated, slope


def sum_body(totals, extras):
    return totals, []


def start_body(totals, extras):
    states, encoder, upstream, gain = extras
    normed, scale = norm_forward(states.astype(jnp.float32), gain)
    return [scale], [normed, encoder, upstream]


def forward_body(totals, extras):
    before, gain = extras
    rows = before + totals[0]
    normed, scale = norm_forward(rows, gain)
    return [rows, scale], [normed]


def backward_body(totals, extras):
    rows, scale, gain, upper = extras[:4]
    step_grad, gain_grad = norm_backward(rows, scale, gain, totals[0])
    rows_grad = upper.astype(jnp.float32) + step_grad
    return [rows_grad, gain_grad] + totals[1:], [rows_grad.astype(jnp.bfloat16)]


def last_body(totals, extras):
    states, scale, gain, upper, small = extras
    rows = states.astype(jnp.float32)
    step_grad, gain_grad = norm_backward(rows, scale, gain, totals[0])
    place = lax.broadcasted_iota(jnp.int32, small.shape, 1)
    return [upper + step_grad], [jnp.where(place == 0, gain_grad, small)]


def gather_weight(pieces):
    return lax.all_gather(jnp.concatenate(pieces, 1), "dp", axis=0, tiled=True)


def scatter_weight(pieces):
    whole = jnp.concatenate(pieces, 1).astype(jnp.bfloat16)
    return lax.psum_scatter(whole, "dp", scatter_dimension=0, tiled=True).astype(jnp.float32)


def forward_product(rows, weight):
    return lax.dot_general(
        rows, weight, (((2,), (0,)), ((), ())), preferred_element_type=jnp.float32
    )


def back_product(rows, weight):
    return lax.dot_general(
        rows, weight, (((2,), (1,)), ((), ())), preferred_element_type=jnp.float32
    )


def weight_product(rows, gradient):
    return lax.dot_general(
        rows, gradient, (((0, 1), (0, 1)), ((), ())), preferred_element_type=jnp.float32
    )


def cut_columns(value, widths):
    parts, at = [], 0
    for width in widths:
        parts.append(value[..., at : at + width])
        at += width
    return parts


def on_device(
    states,
    encoder,
    upstream,
    decoder_docs,
    encoder_docs,
    norm_self,
    norm_cross,
    norm_feed,
    position_table,
    self_query,
    self_key,
    self_value,
    self_output,
    cross_query,
    cross_key,
    cross_value,
    cross_output,
    feed_gate,
    feed_up,
    feed_down,
):
    parts, _, width = states.shape
    length = decoder_docs.shape[1]
    encoder_length = encoder_docs.shape[1]
    inner = self_query.shape[1]
    hidden = feed_gate.shape[1]
    heads = inner // HEAD_DIM
    block = 256
    low = jnp.bfloat16

    attention = gather_weight(
        [
            self_query,
            self_key,
            self_value,
            self_output.T,
            cross_query,
            cross_key,
            cross_value,
            cross_output.T,
        ]
    )
    self_in, middle = cut_columns(attention, (3 * inner, 5 * inner))
    feed = gather_weight([feed_gate, feed_up, feed_down.T])
    self_out, query_cross, both_cross, cross_out = cut_columns(
        middle, (inner, inner, 2 * inner, inner)
    )
    feed_in, feed_out = cut_columns(feed, (2 * hidden, hidden))

    tensor_index = lax.axis_index("tensor")
    table = lax.dynamic_slice_in_dim(position_table, tensor_index * heads, heads, 1).T
    docs_column = decoder_docs[:, :, None]
    docs_row = decoder_docs[:, None, :]
    encoder_row = encoder_docs[:, None, :]

    residual = states.astype(jnp.float32)
    rows_shape = jax.ShapeDtypeStruct(states.shape, jnp.float32)
    encoder_shape = jax.ShapeDtypeStruct(encoder.shape, jnp.float32)
    scale_shape = jax.ShapeDtypeStruct(states.shape[:2] + (1,), jnp.float32)
    gain_shape = jax.ShapeDtypeStruct((1, 1, width), jnp.float32)
    gain_self, gain_cross, gain_feed = (
        gain.reshape(1, 1, width) for gain in (norm_self, norm_cross, norm_feed)
    )
    scale_self, whole_self, encoder_whole, upper = exchange(
        0,
        start_body,
        [],
        [states, encoder, upstream, gain_self],
        [scale_shape],
        [states, encoder, upstream],
    )

    qkv = forward_product(whole_self, self_in).astype(low)
    log_shape = jax.ShapeDtypeStruct((parts, length, heads), jnp.float32)
    mixed_shape = jax.ShapeDtypeStruct((parts, length, inner), low)
    self_mixed, self_log = per_sequence(
        functools.partial(self_forward_kernel, heads, block),
        table,
        (docs_column, docs_row, qkv),
        (mixed_shape, log_shape),
    )
    residual_one, scale_cross, whole_cross = exchange(
        1,
        forward_body,
        [back_product(self_mixed, self_out).astype(low)],
        [residual, gain_cross],
        [rows_shape, scale_shape],
        [states],
    )
    both = forward_product(encoder_whole, both_cross).astype(low)
    queries = forward_product(whole_cross, query_cross).astype(low)
    cross_mixed, cross_log = per_sequence(
        functools.partial(cross_forward_kernel, heads, block),
        None,
        (docs_column, encoder_row, queries, both),
        (mixed_shape, log_shape),
    )
    residual_two, scale_feed, whole_feed = exchange(
        2,
        forward_body,
        [back_product(cross_mixed, cross_out).astype(low)],
        [residual_one, gain_feed],
        [rows_shape, scale_shape],
        [states],
    )
    gate, upward = cut_columns(forward_product(whole_feed, feed_in), (hidden, hidden))
    activated, slope = gelu_parts(gate)
    hidden_state = (activated * upward).astype(low)
    feed_result = back_product(hidden_state, feed_out).astype(low)

    hidden_grad = forward_product(upper, feed_out)
    gate_grad = (hidden_grad * upward * slope).astype(low)
    up_grad = (hidden_grad * activated).astype(low)
    both_grad = jnp.concatenate([gate_grad, up_grad], 2)
    feed_weights = scatter_weight(
        [weight_product(whole_feed, both_grad), weight_product(upper, hidden_state)]
    )
    grad_two, norm_feed_gradient, feed_total, upper_two = exchange(
        3,
        backward_body,
        [back_product(both_grad, feed_in).astype(low), feed_result],
        [residual_two, scale_feed, gain_feed, upstream],
        [rows_shape, gain_shape, rows_shape],
        [states],
    )
    layer_output = (residual_two + feed_total).astype(low)

    mixed_grad = forward_product(upper_two, cross_out).astype(low)
    query_grad, both_grad = per_sequence(
        functools.partial(cross_backward_kernel, heads, block),
        None,
        (docs_column, encoder_row, queries, both, cross_log, mixed_grad),
        (mixed_shape, jax.ShapeDtypeStruct((parts, encoder_length, 2 * inner), low)),
    )
    cross_query_whole = weight_product(whole_cross, query_grad)
    cross_both_whole = weight_product(encoder_whole, both_grad)
    cross_output_whole = weight_product(upper_two, cross_mixed)
    grad_one, norm_cross_gradient, encoder_total, upper_one = exchange(
        4,
        backward_body,
        [
            back_product(query_grad, query_cross).astype(low),
            back_product(both_grad, both_cross).astype(low),
        ],
        [residual_one, scale_cross, gain_cross, grad_two],
        [rows_shape, gain_shape, encoder_shape],
        [states],
    )
    encoder_gradient = encoder_total + 0.0
    self_output_whole = weight_product(upper_one, self_mixed)
    mixed_grad = forward_product(upper_one, self_out).astype(low)
    qkv_grad, diagonal = per_sequence(
        functools.partial(self_backward_kernel, heads, block),
        table,
        (docs_column, docs_row, qkv, self_log, mixed_grad),
        (
            jax.ShapeDtypeStruct((parts, length, 3 * inner), low),
            jax.ShapeDtypeStruct((parts, heads, 2 * block), jnp.float32),
        ),
    )
    count = distance_buckets(window_distance((1, 2 * block), 2 * block, block))
    onehot = (count == jnp.arange(BUCKETS, dtype=jnp.int32)[:, None]).astype(jnp.float32)
    table_local = jnp.dot(onehot, jnp.sum(diagonal, 0).T, precision=lax.Precision.HIGHEST)
    table_full = lax.dynamic_update_slice_in_dim(
        jnp.zeros(position_table.shape, jnp.float32), table_local, tensor_index * heads, 1
    )
    table_flat = table_full.reshape(1, 1, -1)
    table_row = jnp.pad(table_flat, ((0, 0), (0, 0), (0, width - table_flat.shape[2])))
    small = jnp.concatenate(
        [
            jnp.zeros((1, 1, width), jnp.float32),
            norm_cross_gradient,
            norm_feed_gradient,
            table_row,
            jnp.zeros((1, 4, width), jnp.float32),
        ],
        1,
    )
    states_gradient, small = exchange(
        5,
        last_body,
        [back_product(qkv_grad, self_in).astype(low)],
        [states, scale_self, gain_self, grad_one, small],
        [rows_shape],
        [small],
    )
    small = jnp.sum(small.reshape(4, 8, width), 0)
    rest = jnp.concatenate(
        [
            self_output_whole,
            cross_query_whole,
            cross_both_whole,
            cross_output_whole,
            weight_product(whole_self, qkv_grad),
        ],
        1,
    ).astype(low)
    rest, small = spread_sum(6, width // self_query.shape[0], rest, small)
    middle_weights, self_weights = rest[:, : 5 * inner], rest[:, 5 * inner :]

    query_self_g, key_self_g, value_self_g = cut_columns(self_weights, (inner,) * 3)
    self_out_g, query_cross_g, key_cross_g, value_cross_g, cross_out_g = cut_columns(
        middle_weights, (inner,) * 5
    )
    gate_g, up_g, down_g = cut_columns(feed_weights, (hidden,) * 3)
    return (
        layer_output,
        states_gradient,
        encoder_gradient,
        small[0],
        small[1],
        small[2],
        small[3, : position_table.size].reshape(position_table.shape),
        query_self_g,
        key_self_g,
        value_self_g,
        self_out_g.T,
        query_cross_g,
        key_cross_g,
        value_cross_g,
        cross_out_g.T,
        gate_g,
        up_g,
        down_g.T,
    )


def solution(mesh):
    return jax.shard_map(
        on_device,
        mesh=mesh,
        in_specs=(
            P("dp", "tensor", None),
            P("dp", "tensor", None),
            P("dp", "tensor", None),
            P("dp", None),
            P("dp", None),
            P(),
            P(),
            P(),
            P(),
            P("dp", "tensor"),
            P("dp", "tensor"),
            P("dp", "tensor"),
            P("tensor", "dp"),
            P("dp", "tensor"),
            P("dp", "tensor"),
            P("dp", "tensor"),
            P("tensor", "dp"),
            P("dp", "tensor"),
            P("dp", "tensor"),
            P("tensor", "dp"),
        ),
        out_specs=(
            P("dp", "tensor", None),
            P("dp", "tensor", None),
            P("dp", "tensor", None),
            P(),
            P(),
            P(),
            P(),
            P("dp", "tensor"),
            P("dp", "tensor"),
            P("dp", "tensor"),
            P("tensor", "dp"),
            P("dp", "tensor"),
            P("dp", "tensor"),
            P("dp", "tensor"),
            P("tensor", "dp"),
            P("dp", "tensor"),
            P("dp", "tensor"),
            P("tensor", "dp"),
        ),
        check_vma=False,
    )
```
